32 devices in a mesh: blk: 8 (over y, x, core), uly: 4 (over z).
Axes of the slice: x: 2, y: 2, z: 4, core: 2. Of those that a mesh axis runs over, the one named last changes fastest.
Arguments:
- q_code: bfloat16 [16384, 6144], P(('blk', 'uly')), may hold values from -6 to 6
- k_code: bfloat16 [16384, 6144], P(('blk', 'uly')), may hold values from -4 to 4
- v_code: bfloat16 [16384, 6144], P(('blk', 'uly')), may hold values from -6 to 6
- block_exp: int32 [128, 3, 48], P(('blk', 'uly')), may hold values from -2 to 1
- window: int32 [128, 27], P('blk'), may hold values from 0 to 47, as said below
- window_count: int32 [128], P('blk'), may hold values from 9 to 27, as said below
Outputs:
- attn_out: bfloat16 [16384, 6144], P(('blk', 'uly'))
The draws below stay inside these ranges and needn't reach their ends.
Inputs may be any that keep to these rules, and one draw needn't show every extreme that they name: `window`: for s < window_count[g] the slots name distinct tiles in groups of nine: each group a 3 x 3 block of the 4 x 4 tile grid of one frame; the first group lies in the query's own frame and holds the query's own tile, the others in the frame before or after; no group reaches before the first frame or after the last. Unused slots hold some tile of the own frame. `window_count`: A multiple of 9.
All inputs are finite; a program needn't handle non-finite values.
Results may differ from the reference program's by a relative error of at most 0.0027.
Values may be sent and summed in bfloat16 or wider, within the bound.
No kernel may reach another device: no remote copies, remote signals or barrier semaphores. Data moves between devices by JAX's collectives and lax.ppermute only.
A program may use at most 192 MiB of HBM per device.

```python
import math
import jax
import jax.numpy as jnp
from jax import lax

D = 6144
HEADS = 48
HEAD_DIM = 128
TILE = 128
TILE_ROWS = 4
TILE_COLS = 4
NBR = 27
FRAME_TILES = 16
TILES = 128
TOKENS = 16384
N_BLK = 8


def draw_q_code(key, part):
    key = jax.random.fold_in(key, 21)
    return jnp.clip(1.5 * jax.random.normal(key, (TOKENS, D), jnp.float32), -6.0, 6.0).astype(jnp.bfloat16)


def draw_k_code(key, part):
    key = jax.random.fold_in(key, 22)
    return jnp.clip(jax.random.normal(key, (TOKENS, D), jnp.float32), -4.0, 4.0).astype(jnp.bfloat16)


def window_plan(key):
    tile_id = jnp.arange(TILES, dtype=jnp.int32)
    frame_id = tile_id // FRAME_TILES
    inside = tile_id % FRAME_TILES
    tile_row = inside // TILE_COLS
    tile_col = inside % TILE_COLS
    shifts = jax.random.randint(jax.random.fold_in(key, 5), (TILES, 3, 2), -1, 2)
    row_start = jnp.clip(tile_row[:, None] - 1 + shifts[:, :, 0], 0, TILE_ROWS - 3)
    col_start = jnp.clip(tile_col[:, None] - 1 + shifts[:, :, 1], 0, TILE_COLS - 3)
    row_offset = jnp.array([0, 0, 0, 1, 1, 1, 2, 2, 2], jnp.int32)
    col_offset = jnp.array([0, 1, 2, 0, 1, 2, 0, 1, 2], jnp.int32)
    frame_slot = jnp.arange(3, dtype=jnp.int32)[None, :, None]
    window_tiles = frame_slot * FRAME_TILES + (row_start[:, :, None] + row_offset) * TILE_COLS + col_start[:, :, None] + col_offset
    coin_flips = jax.random.randint(jax.random.fold_in(key, 6), (TILES, 2), 0, 4)
    forced = tile_id == FRAME_TILES
    use_prev = (coin_flips[:, 0] > 0) & (frame_id > 0) | forced
    use_next = (coin_flips[:, 1] > 0) & (frame_id < N_BLK - 1) | forced
    second = jnp.where(use_prev[:, None], window_tiles[:, 0], window_tiles[:, 2])
    second = jnp.where((use_prev | use_next)[:, None], second, window_tiles[:, 1])
    third_group = jnp.where((use_prev & use_next)[:, None], window_tiles[:, 2], window_tiles[:, 1])
    slot_table = jnp.concatenate([window_tiles[:, 1], second, third_group], axis=1).astype(jnp.int32)
    live_slots = (9 * (1 + use_prev.astype(jnp.int32) + use_next.astype(jnp.int32))).astype(jnp.int32)
    return (slot_table, live_slots)


def draw_window(key, part):
    slot_table, live_slots = window_plan(key)
    return slot_table


def draw_window_count(key, part):
    slot_table, live_slots = window_plan(key)
    return live_slots


def touch_ends(values, key, least, high):
    place = [jax.random.randint(jax.random.fold_in(key, axis), (), 0, length) for axis, length in enumerate(values.shape)]
    widest = values.shape.index(max(values.shape))
    beside = place[:widest] + [(place[widest] + 1) % values.shape[widest]] + place[widest + 1:]
    return values.at[tuple(place)].set(least).at[tuple(beside)].set(high)


def block_levels(rng, dims, split, low, top_value):
    def one(dim, parts):
        steps = jax.random.uniform(jax.random.fold_in(jax.random.fold_in(rng, 6), dim), (parts,), jnp.float32, low / len(split), top_value / len(split))
        return jnp.repeat(jnp.exp(steps), dims[dim] // parts).reshape((-1,) + (1,) * (len(dims) - dim - 1))

    factor_of = one(*split[0])
    for cut in split[1:]:
        factor_of = factor_of * one(*cut)
    return factor_of


def normal_values(rng, extent, deviation, bound, shards=(), kind=jnp.bfloat16):
    values = jax.random.normal(rng, extent, jnp.float32) * deviation
    if len(shards) > 0:
        values = block_levels(rng, extent, shards, -0.22, 0.18) * values
    return jnp.clip(values, min=-bound, max=bound).astype(kind)


def setup_inputs(seed: int = 0) -> dict:
    keys = jax.random.split(jax.random.key(seed), 7)
    return {
        "q_code": draw_q_code(jax.random.fold_in(keys[6], 71), 0),
        "k_code": draw_k_code(jax.random.fold_in(keys[6], 71), 0),
        "v_code": normal_values(keys[2], (TOKENS, D), 1.0, 6.0, ((0, 32),)),
        "block_exp": touch_ends(jax.random.randint(keys[3], (TILES, 3, HEADS), -2, 2), jax.random.fold_in(keys[3], 1), -2, 1).astype(jnp.int32),
        "window": draw_window(jax.random.fold_in(keys[6], 71), 0),
        "window_count": draw_window_count(jax.random.fold_in(keys[6], 71), 0),
    }


def hadamard(order):
    indices = jnp.arange(order, dtype=jnp.int32)
    common = indices[:, None] & indices[None, :]
    parity = jnp.zeros((order, order), jnp.int32)
    for bit_pos in range(max(1, order.bit_length())):
        parity = parity + (common >> bit_pos & 1)
    signs = jnp.where(parity % 2 == 0, 1.0, -1.0).astype(jnp.float32)
    return signs / math.sqrt(order)

def dequantize(code, exponent, tile_len, head_count):
    row_total, model_width = code.shape
    factor = jnp.exp2(exponent.astype(jnp.float32)).astype(jnp.bfloat16)
    blocks = code.reshape(row_total // tile_len, tile_len, head_count, model_width // head_count)
    return blocks * factor[:, None, :, None]

def reference(q_code, k_code, v_code, block_exp, window, window_count):
    queries = dequantize(q_code, block_exp[:, 0], TILE, HEADS).reshape(N_BLK, FRAME_TILES, TILE, HEADS, HEAD_DIM)
    key_rows = dequantize(k_code, block_exp[:, 1], TILE, HEADS).reshape(N_BLK, FRAME_TILES, TILE, HEADS, HEAD_DIM)
    value_rows = dequantize(v_code, block_exp[:, 2], TILE, HEADS).reshape(N_BLK, FRAME_TILES, TILE, HEADS, HEAD_DIM)
    empty = jnp.zeros((1, FRAME_TILES, TILE, HEADS, HEAD_DIM), jnp.bfloat16)
    key_pad = jnp.concatenate([empty, key_rows, empty], axis=0)
    value_pad = jnp.concatenate([empty, value_rows, empty], axis=0)
    slot_table = window.reshape(N_BLK, FRAME_TILES, NBR)
    live_table = window_count.reshape(N_BLK, FRAME_TILES)
    rotation = hadamard(HEAD_DIM)
    inv_root = 1.0 / math.sqrt(HEAD_DIM)

    def one_frame(frame_id):
        key_ext = lax.dynamic_slice_in_dim(key_pad, frame_id, 3, 0).reshape(3 * FRAME_TILES, TILE, HEADS, HEAD_DIM)
        value_ext = lax.dynamic_slice_in_dim(value_pad, frame_id, 3, 0).reshape(3 * FRAME_TILES, TILE, HEADS, HEAD_DIM)
        index_table = lax.dynamic_index_in_dim(slot_table, frame_id, 0, False)
        live_slots = lax.dynamic_index_in_dim(live_table, frame_id, 0, False)
        valid_slot = jnp.arange(NBR, dtype=jnp.int32)[None, :] < live_slots[:, None]
        query_frame = lax.dynamic_index_in_dim(queries, frame_id, 0, False)

        def one_head(head_idx):
            query_head = lax.dynamic_index_in_dim(query_frame, head_idx, 2, False)
            key_head = lax.dynamic_index_in_dim(key_ext, head_idx, 2, False)
            value_head = lax.dynamic_index_in_dim(value_ext, head_idx, 2, False)
            key_tiles = jnp.take(key_head, index_table, axis=0)
            value_tiles = jnp.take(value_head, index_table, axis=0)
            scores = jnp.einsum('gqd,gnkd->gqnk', query_head.astype(jnp.float32), key_tiles.astype(jnp.float32)) * inv_root
            scores = jnp.where(valid_slot[:, None, :, None], scores, -jnp.inf)
            largest = lax.optimization_barrier(jnp.max(scores, axis=(2, 3), keepdims=True))
            expsum = jnp.exp(scores - largest)
            totals = lax.optimization_barrier(jnp.sum(expsum, axis=(2, 3)))
            weights = lax.optimization_barrier(expsum.astype(jnp.bfloat16))
            summed = jnp.einsum('gqnk,gnkd->gqd', weights.astype(jnp.float32), value_tiles.astype(jnp.float32))
            rotated = summed / totals[:, :, None]
            result = jnp.einsum('gqd,de->gqe', rotated, rotation, precision=lax.Precision.HIGHEST)
            return result.astype(jnp.bfloat16)
        per_head = lax.map(one_head, jnp.arange(HEADS, dtype=jnp.int32))
        return jnp.transpose(per_head, (1, 2, 0, 3))
    frames = lax.map(one_frame, jnp.arange(N_BLK, dtype=jnp.int32))
    return frames.reshape(TOKENS, D)
```

```python
import math

import jax
import jax.numpy as jnp
from jax import lax
from jax.experimental import pallas as pl
from jax.experimental.pallas import tpu as pltpu
from jax.sharding import PartitionSpec as P

LOG2E = math.log2(math.e)
ANYWHERE = pl.BlockSpec(memory_space=pl.ANY)
GROUP = 9
VMEM = 60 << 20


def hadamard_signs(order):
    indices = jnp.arange(order, dtype=jnp.int32)
    common = indices[:, None] & indices[None, :]
    parity = jnp.zeros((order, order), jnp.int32)
    for bit_pos in range(max(1, order.bit_length())):
        parity = parity + (common >> bit_pos & 1)
    return jnp.where(parity % 2 == 0, 1.0, -1.0).astype(jnp.bfloat16)


def chunk_sizes(local_heads):
    if local_heads % 12 == 0:
        unit = local_heads // 12
        return [unit * size for size in (2, 2, 2, 2, 2, 1, 1)]
    return [1] * local_heads


def params():
    return pltpu.CompilerParams(vmem_limit_bytes=VMEM)


def light():
    return pl.CostEstimate(flops=0, bytes_accessed=1 << 20, transcendentals=0)


def pack(z, factor, q_code, k_code, v_code, first, heads, local_heads, width, ulysses, tile, after):
    rows = q_code.shape[0]

    def body(z_ref, factor_ref, *refs):
        codes = refs[: 3 * ulysses]
        outs = refs[-ulysses:]
        for k in range(ulysses):
            head = (z_ref[0] ^ k) * local_heads + first + pl.program_id(0)
            for part, column in enumerate((1, 2, 0)):
                for i in range(rows // tile):
                    span = slice(i * tile, (i + 1) * tile)
                    block = codes[3 * k + part][span, :].astype(jnp.float32) * factor_ref[i, column, head]
                    outs[k][part, span, :] = block.astype(jnp.bfloat16)

    in_specs = [pl.BlockSpec(memory_space=pltpu.SMEM)]
    operands = [factor]
    for k in range(ulysses):
        spec = pl.BlockSpec((rows, width), lambda h, z_ref, k=k: (0, (z_ref[0] ^ k) * local_heads + first + h))
        in_specs += [spec] * 3
        operands += [k_code, v_code, q_code]
    return pl.pallas_call(
        body,
        grid_spec=pltpu.PrefetchScalarGridSpec(
            num_scalar_prefetch=1,
            grid=(heads,),
            in_specs=in_specs + [ANYWHERE] * len(after),
            out_specs=[pl.BlockSpec((3, None, rows, width), lambda h, z_ref: (0, h, 0, 0))] * ulysses,
        ),
        out_shape=[jax.ShapeDtypeStruct((3, heads, rows, width), jnp.bfloat16)] * ulysses,
        compiler_params=params(),
        cost_estimate=light(),
        name="pack",
    )(z, *operands, *after)


def join(pieces, after):
    count = len(pieces)
    _, heads, rows, width = pieces[0].shape

    def body(*refs):
        out = refs[-1]
        for k in range(count):
            out[pl.ds(k * rows, rows), :] = refs[k][...]

    return pl.pallas_call(
        body,
        grid=(heads, 2),
        in_specs=[pl.BlockSpec((None, None, rows, width), lambda h, p: (p, h, 0, 0))] * count
        + [ANYWHERE] * len(after),
        out_specs=pl.BlockSpec((None, None, count * rows, width), lambda h, p: (h, p, 0, 0)),
        out_shape=jax.ShapeDtypeStruct((heads, 2, count * rows, width), jnp.bfloat16),
        compiler_params=params(),
        cost_estimate=light(),
        name="join",
    )(*pieces, *after)


def collect(z, returned, firsts, local_heads, tile):
    ulysses = len(returned[0])
    _, rows, width = returned[0][0].shape
    model_width = ulysses * local_heads * width
    pieces = [(c, k) for c in range(len(returned)) for k in range(ulysses)]

    def body(z_ref, *refs):
        out = refs[-1]
        for ref, (c, k) in zip(refs, pieces):
            for h in range(ref.shape[0]):
                column = ((z_ref[0] ^ k) * local_heads + firsts[c] + h) * width
                out[:, pl.ds(pl.multiple_of(column, width), width)] = ref[h]

    return pl.pallas_call(
        body,
        grid_spec=pltpu.PrefetchScalarGridSpec(
            num_scalar_prefetch=1,
            grid=(rows // tile,),
            in_specs=[
                pl.BlockSpec((returned[c][k].shape[0], tile, width), lambda i, z_ref: (0, i, 0))
                for c, k in pieces
            ],
            out_specs=pl.BlockSpec((tile, model_width), lambda i, z_ref: (i, 0)),
        ),
        out_shape=jax.ShapeDtypeStruct((rows, model_width), jnp.bfloat16),
        compiler_params=params(),
        cost_estimate=light(),
        name="collect",
    )(z, *[returned[c][k] for c, k in pieces])


def unit_table(window, window_count, z, per_piece, group):
    frame_tiles, slot_total = window.shape
    groups = window_count // group
    ends = jnp.cumsum(groups)
    unit = jnp.arange(frame_tiles * (slot_total // group) + 4, dtype=jnp.int32)
    owner = jnp.sum(unit[:, None] >= ends[None, :], axis=1).astype(jnp.int32)
    order = jnp.minimum(unit - (ends - groups)[jnp.minimum(owner, frame_tiles - 1)], slot_total // group - 1)

    def placed(tiles):
        frame, inside = tiles // frame_tiles, tiles % frame_tiles
        return frame * frame_tiles + ((inside // per_piece) ^ z) * per_piece + inside % per_piece

    members = placed(window).reshape(frame_tiles, slot_total // group, group)
    members = members[jnp.minimum(owner, frame_tiles - 1), order]
    spare = owner >= frame_tiles
    own = jnp.where(spare, frame_tiles, placed(jnp.minimum(owner, frame_tiles - 1)))
    first = (order == 0) | spare
    head = jnp.stack([own, first.astype(jnp.int32)], axis=1)
    return jnp.concatenate([head, members], axis=1).reshape(-1), ends[-1:]


def attend(z, units, unit_count, signs, queries, before, current, later, width, tile, group, after):
    ulysses = len(queries)
    heads, _, frame_rows, _ = current.shape
    rows = frame_rows // ulysses
    frame_tiles = frame_rows // tile
    span = group * tile
    stride = group + 2
    lag, ring = 3, 4
    to_log2 = LOG2E / math.sqrt(width)
    post = 1.0 / math.sqrt(width)

    def body(unit_ref, count_ref, signs_ref, *refs):
        query_refs = refs[:ulysses]
        frames = refs[ulysses : ulysses + 3]
        refs = refs[ulysses + 3 + len(after) :]
        outs = refs[:ulysses]
        keys, values, query_all, tops, total_all, sum_all = refs[ulysses : ulysses + 6]
        scores = refs[ulysses + 6 :]
        count = count_ref[0]
        for k in range(ulysses):
            query_all[pl.ds(k * rows, rows), :] = query_refs[k][...]
        for f in range(3):
            values[pl.ds(f * frame_rows, frame_rows), :] = frames[f][1]
            keys[pl.ds(f * frame_rows, frame_rows), :] = frames[f][0]
        total_all[...] = jnp.zeros_like(total_all)
        sum_all[...] = jnp.zeros_like(sum_all)

        def tiles_of(source, u):
            parts = []
            for s in range(group):
                start = pl.multiple_of(unit_ref[u * stride + 2 + s] * tile, tile)
                parts.append(source[pl.ds(start, tile), :])
            return jnp.concatenate(parts, axis=0)

        def score(u, slot):
            t = unit_ref[u * stride]
            query = query_all[pl.ds(pl.multiple_of(t * tile, tile), tile), :]
            block = lax.dot_general(
                query, tiles_of(keys, u), (((1,), (1,)), ((), ())), preferred_element_type=jnp.float32
            )
            scores[slot][...] = block
            top = block[:, :tile]
            for s in range(1, group):
                top = jnp.maximum(top, block[:, s * tile : (s + 1) * tile])
            known = tops[t]
            tops[t] = jnp.where(unit_ref[u * stride + 1] == 1, top, jnp.maximum(top, known))

        def weigh(u, slot, top):
            t = unit_ref[u * stride]
            expo = jnp.exp2(scores[slot][...] * to_log2 - top)
            total = expo[:, :tile]
            for s in range(1, group):
                total = total + expo[:, s * tile : (s + 1) * tile]
            total_all[t] += total
            sum_all[t] += lax.dot_general(
                expo.astype(jnp.bfloat16),
                tiles_of(values, u),
                (((1,), (0,)), ((), ())),
                preferred_element_type=jnp.float32,
            )

        for u in range(lag):
            score(u, u)

        def four_units(i, carry):
            for j in range(ring):
                u = i * ring + j
                top = jnp.max(tops[unit_ref[u * stride]], axis=1, keepdims=True) * to_log2
                score(u + lag, (j + lag) % ring)
                weigh(u, j, top)
            return carry

        lax.fori_loop(0, (count + ring - 1) // ring, four_units, 0)
        for k in range(ulysses):
            for i in range(rows // tile):
                t = k * (rows // tile) + i
                rotated = sum_all[t] * (post / jnp.sum(total_all[t], axis=1, keepdims=True))
                high = rotated.astype(jnp.bfloat16)
                rest = rotated - high.astype(jnp.float32)
                middle = rest.astype(jnp.bfloat16)
                low = (rest - middle.astype(jnp.float32)).astype(jnp.bfloat16)
                signs_val = signs_ref[...]
                result = jnp.dot(low, signs_val, preferred_element_type=jnp.float32)
                result += jnp.dot(middle, signs_val, preferred_element_type=jnp.float32)
                result += jnp.dot(high, signs_val, preferred_element_type=jnp.float32)
                outs[k][pl.ds(i * tile, tile), :] = result.astype(jnp.bfloat16)

    frame_spec = pl.BlockSpec((None, 2, frame_rows, width), lambda h, *_: (h, 0, 0, 0))
    return pl.pallas_call(
        body,
        grid_spec=pltpu.PrefetchScalarGridSpec(
            num_scalar_prefetch=2,
            grid=(heads,),
            in_specs=[pl.BlockSpec((width, width), lambda h, *_: (0, 0))]
            + [pl.BlockSpec((None, None, rows, width), lambda h, *_: (2, h, 0, 0))] * ulysses
            + [frame_spec] * 3
            + [ANYWHERE] * len(after),
            out_specs=[pl.BlockSpec((None, rows, width), lambda h, *_: (h, 0, 0))] * ulysses,
            scratch_shapes=[
                pltpu.VMEM((3 * frame_rows, width), jnp.bfloat16),
                pltpu.VMEM((3 * frame_rows, width), jnp.bfloat16),
                pltpu.VMEM((frame_rows + tile, width), jnp.bfloat16),
                pltpu.VMEM((frame_tiles + 1, tile, tile), jnp.float32),
                pltpu.VMEM((frame_tiles + 1, tile, tile), jnp.float32),
                pltpu.VMEM((frame_tiles + 1, tile, width), jnp.float32),
            ]
            + [pltpu.VMEM((tile, span), jnp.float32)] * ring,
        ),
        out_shape=[jax.ShapeDtypeStruct((heads, rows, width), jnp.bfloat16)] * ulysses,
        compiler_params=pltpu.CompilerParams(vmem_limit_bytes=60 << 20),
        cost_estimate=pl.CostEstimate(flops=0, bytes_accessed=1 << 20, transcendentals=0),
        name="attend",
    )(units, unit_count, signs, *queries, before, current, later, *after)


def across(block, step):
    size = lax.axis_size("uly")
    return lax.ppermute(block, "uly", [(i, i ^ step) for i in range(size)])


def from_behind(block, distance):
    devices = range(lax.axis_size("blk"))
    route = [(i - distance, i) for i in devices if i - distance in devices]
    return lax.ppermute(block, "blk", route)


def shards(q_code, k_code, v_code, block_exp, window, window_count):
    rows, model_width = q_code.shape
    tile = rows // block_exp.shape[0]
    head_count = block_exp.shape[2]
    width = model_width // head_count
    ulysses = lax.axis_size("uly")
    local_heads = head_count // ulysses
    place = lax.axis_index("uly").astype(jnp.int32)
    z = place.reshape(1)
    factor = jnp.exp2(block_exp.astype(jnp.float32))
    signs = hadamard_signs(width)
    sizes = chunk_sizes(local_heads)
    firsts = [sum(sizes[:c]) for c in range(len(sizes))]
    steps = len(sizes)
    ahead = 2
    units, unit_count = unit_table(window, window_count, place, rows // tile, GROUP)
    arrived, halos, returned = {}, {}, {}
    last = []

    def send(c):
        nonlocal last
        packed = pack(
            z, factor, q_code, k_code, v_code, firsts[c], sizes[c], local_heads, width, ulysses, tile, last
        )
        last = [packed[0]]
        arrived[c] = [packed[0]] + [across(packed[k], k) for k in range(1, ulysses)]

    def spread(c):
        nonlocal last
        current = join(arrived[c], last)
        last = [current]
        halos[c] = (from_behind(current, 1), current, from_behind(current, -1))

    def compute(c):
        nonlocal last
        mixed = attend(z, units, unit_count, signs, arrived[c], *halos[c], width, tile, GROUP, last)
        last = [mixed[0]]
        returned[c] = [mixed[0]] + [across(mixed[k], k) for k in range(1, ulysses)]

    for c in range(min(ahead, steps)):
        send(c)
    for c in range(steps):
        spread(c)
        if c + ahead < steps:
            send(c + ahead)
        if c >= 1:
            compute(c - 1)
    compute(steps - 1)
    return collect(z, [returned[c] for c in range(steps)], firsts, local_heads, tile)


def solution(mesh):
    return jax.shard_map(
        shards,
        mesh=mesh,
        in_specs=(
            P(("blk", "uly"), None),
            P(("blk", "uly"), None),
            P(("blk", "uly"), None),
            P(("blk", "uly"), None, None),
            P("blk", None),
            P("blk"),
        ),
        out_specs=P(("blk", "uly"), None),
        check_vma=False,
    )
```

```python
import math

import jax
import jax.numpy as jnp
from jax import lax
from jax.experimental import pallas as pl
from jax.experimental.pallas import tpu as pltpu
from jax.sharding import PartitionSpec as P

LOG2E = math.log2(math.e)
ANYWHERE = pl.BlockSpec(memory_space=pl.ANY)
GROUP = 9
VMEM = 60 << 20
SIZES = (2, 2, 2, 2, 2, 2)
BACK = (4, 2)
AHEAD = 2


def hadamard_signs(order):
    indices = jnp.arange(order, dtype=jnp.int32)
    common = indices[:, None] & indices[None, :]
    parity = jnp.zeros((order, order), jnp.int32)
    for bit_pos in range(max(1, order.bit_length())):
        parity = parity + (common >> bit_pos & 1)
    return jnp.where(parity % 2 == 0, 1.0, -1.0).astype(jnp.bfloat16)


def cut(local_heads):
    if local_heads % 12 == 0:
        unit = local_heads // 12
        return [unit * size for size in SIZES], BACK
    return [1] * local_heads, [local_heads - 2, 2] if local_heads > 2 else [local_heads]


def params():
    return pltpu.CompilerParams(vmem_limit_bytes=VMEM)


def light():
    return pl.CostEstimate(flops=0, bytes_accessed=1 << 20, transcendentals=0)


def pack(z, factor, q_code, k_code, v_code, first, heads, local_heads, width, ulysses, tile, after):
    rows = q_code.shape[0]

    def body(z_ref, factor_ref, *refs):
        codes = refs[: 3 * ulysses]
        outs = refs[-ulysses:]
        for k in range(ulysses):
            head = (z_ref[0] ^ k) * local_heads + first + pl.program_id(0)
            for part, column in enumerate((1, 2, 0)):
                for i in range(rows // tile):
                    span = slice(i * tile, (i + 1) * tile)
                    block = codes[3 * k + part][span, :].astype(jnp.float32) * factor_ref[i, column, head]
                    outs[k][part, span, :] = block.astype(jnp.bfloat16)

    in_specs = [pl.BlockSpec(memory_space=pltpu.SMEM)]
    operands = [factor]
    for k in range(ulysses):
        spec = pl.BlockSpec((rows, width), lambda h, z_ref, k=k: (0, (z_ref[0] ^ k) * local_heads + first + h))
        in_specs += [spec] * 3
        operands += [k_code, v_code, q_code]
    return pl.pallas_call(
        body,
        grid_spec=pltpu.PrefetchScalarGridSpec(
            num_scalar_prefetch=1,
            grid=(heads,),
            in_specs=in_specs + [ANYWHERE] * len(after),
            out_specs=[pl.BlockSpec((3, None, rows, width), lambda h, z_ref: (0, h, 0, 0))] * ulysses,
        ),
        out_shape=[jax.ShapeDtypeStruct((3, heads, rows, width), jnp.bfloat16)] * ulysses,
        compiler_params=params(),
        cost_estimate=light(),
        name="pack",
    )(z, *operands, *after)


def join(pieces, after):
    count = len(pieces)
    _, heads, rows, width = pieces[0].shape

    def body(*refs):
        out = refs[-1]
        for k in range(count):
            out[pl.ds(k * rows, rows), :] = refs[k][...]

    return pl.pallas_call(
        body,
        grid=(heads, 2),
        in_specs=[pl.BlockSpec((None, None, rows, width), lambda h, p: (p, h, 0, 0))] * count
        + [ANYWHERE] * len(after),
        out_specs=pl.BlockSpec((None, None, count * rows, width), lambda h, p: (h, p, 0, 0)),
        out_shape=jax.ShapeDtypeStruct((heads, 2, count * rows, width), jnp.bfloat16),
        compiler_params=params(),
        cost_estimate=light(),
        name="join",
    )(*pieces, *after)


def collect(z, returned, heads_before, local_heads, tile):
    ulysses = len(returned[0])
    _, rows, width = returned[0][0].shape
    model_width = ulysses * local_heads * width
    pieces = [(c, k) for c in range(len(returned)) for k in range(ulysses)]

    def body(z_ref, *refs):
        out = refs[-1]
        for ref, (c, k) in zip(refs, pieces):
            for h in range(ref.shape[0]):
                column = ((z_ref[0] ^ k) * local_heads + heads_before[c] + h) * width
                out[:, pl.ds(pl.multiple_of(column, width), width)] = ref[h]

    return pl.pallas_call(
        body,
        grid_spec=pltpu.PrefetchScalarGridSpec(
            num_scalar_prefetch=1,
            grid=(rows // tile,),
            in_specs=[
                pl.BlockSpec((returned[c][k].shape[0], tile, width), lambda i, z_ref: (0, i, 0))
                for c, k in pieces
            ],
            out_specs=pl.BlockSpec((tile, model_width), lambda i, z_ref: (i, 0)),
        ),
        out_shape=jax.ShapeDtypeStruct((rows, model_width), jnp.bfloat16),
        compiler_params=params(),
        cost_estimate=light(),
        name="collect",
    )(z, *[returned[c][k] for c, k in pieces])


def unit_table(window, window_count, z, odd, per_piece, group):
    frame_tiles, slot_total = window.shape
    groups = window_count // group
    ends = jnp.cumsum(groups)
    unit = jnp.arange(frame_tiles * (slot_total // group) + 4, dtype=jnp.int32)
    owner = jnp.sum(unit[:, None] >= ends[None, :], axis=1).astype(jnp.int32)
    order = jnp.minimum(unit - (ends - groups)[jnp.minimum(owner, frame_tiles - 1)], slot_total // group - 1)

    def placed(tiles):
        frame, inside = tiles // frame_tiles, tiles % frame_tiles
        slot = jnp.where(frame == 1, 1, jnp.where(odd == 1, frame, 2 - frame))
        return slot * frame_tiles + ((inside // per_piece) ^ z) * per_piece + inside % per_piece

    members = placed(window).reshape(frame_tiles, slot_total // group, group)
    members = members[jnp.minimum(owner, frame_tiles - 1), order]
    spare = owner >= frame_tiles
    inside = jnp.minimum(owner, frame_tiles - 1)
    own = jnp.where(spare, frame_tiles, ((inside // per_piece) ^ z) * per_piece + inside % per_piece)
    first = (order == 0) | spare
    head = jnp.stack([own, first.astype(jnp.int32)], axis=1)
    return jnp.concatenate([head, members], axis=1).reshape(-1), ends[-1:]


def attend(units, unit_count, signs, queries, near, current, far, filled, place, total_heads, width, tile, group, after):
    ulysses = len(queries)
    heads, _, frame_rows, _ = current.shape
    rows = frame_rows // ulysses
    frame_tiles = frame_rows // tile
    span = group * tile
    stride = group + 2
    lag, ring = 3, 4
    to_log2 = LOG2E / math.sqrt(width)
    post = 1.0 / math.sqrt(width)

    def body(unit_ref, count_ref, signs_ref, *refs):
        query_refs = refs[:ulysses]
        frames = refs[ulysses : ulysses + 3]
        refs = refs[ulysses + 3 + len(filled) + len(after) :]
        outs = refs[:ulysses]
        keys, values, query_all, tops, total_all, sum_all = refs[ulysses : ulysses + 6]
        scores = refs[ulysses + 6 :]
        count = count_ref[0]
        for k in range(ulysses):
            query_all[pl.ds(k * rows, rows), :] = query_refs[k][...]
        for f in range(3):
            values[pl.ds(f * frame_rows, frame_rows), :] = frames[f][1]
            keys[pl.ds(f * frame_rows, frame_rows), :] = frames[f][0]
        total_all[...] = jnp.zeros_like(total_all)
        sum_all[...] = jnp.zeros_like(sum_all)

        def tiles_of(source, u):
            parts = []
            for s in range(group):
                start = pl.multiple_of(unit_ref[u * stride + 2 + s] * tile, tile)
                parts.append(source[pl.ds(start, tile), :])
            return jnp.concatenate(parts, axis=0)

        def score(u, slot):
            t = unit_ref[u * stride]
            query = query_all[pl.ds(pl.multiple_of(t * tile, tile), tile), :]
            block = lax.dot_general(
                query, tiles_of(keys, u), (((1,), (1,)), ((), ())), preferred_element_type=jnp.float32
            )
            scores[slot][...] = block
            top = block[:, :tile]
            for s in range(1, group):
                top = jnp.maximum(top, block[:, s * tile : (s + 1) * tile])
            known = tops[t]
            tops[t] = jnp.where(unit_ref[u * stride + 1] == 1, top, jnp.maximum(top, known))

        def weigh(u, slot, top):
            t = unit_ref[u * stride]
            expo = jnp.exp2(scores[slot][...] * to_log2 - top)
            total = expo[:, :tile]
            for s in range(1, group):
                total = total + expo[:, s * tile : (s + 1) * tile]
            total_all[t] += total
            sum_all[t] += lax.dot_general(
                expo.astype(jnp.bfloat16),
                tiles_of(values, u),
                (((1,), (0,)), ((), ())),
                preferred_element_type=jnp.float32,
            )

        for u in range(lag):
            score(u, u)

        def four_units(i, carry):
            for j in range(ring):
                u = i * ring + j
                top = jnp.max(tops[unit_ref[u * stride]], axis=1, keepdims=True) * to_log2
                score(u + lag, (j + lag) % ring)
                weigh(u, j, top)
            return carry

        lax.fori_loop(0, (count + ring - 1) // ring, four_units, 0)
        for k in range(ulysses):
            for i in range(rows // tile):
                t = k * (rows // tile) + i
                rotated = sum_all[t] * (post / jnp.sum(total_all[t], axis=1, keepdims=True))
                high = rotated.astype(jnp.bfloat16)
                rest = rotated - high.astype(jnp.float32)
                middle = rest.astype(jnp.bfloat16)
                low = (rest - middle.astype(jnp.float32)).astype(jnp.bfloat16)
                signs_val = signs_ref[...]
                result = jnp.dot(low, signs_val, preferred_element_type=jnp.float32)
                result += jnp.dot(middle, signs_val, preferred_element_type=jnp.float32)
                result += jnp.dot(high, signs_val, preferred_element_type=jnp.float32)
                outs[k][pl.ds(i * tile, tile), :] = result.astype(jnp.bfloat16)

    frame_spec = pl.BlockSpec((None, 2, frame_rows, width), lambda h, *_: (h, 0, 0, 0))
    return pl.pallas_call(
        body,
        grid_spec=pltpu.PrefetchScalarGridSpec(
            num_scalar_prefetch=2,
            grid=(heads,),
            in_specs=[pl.BlockSpec((width, width), lambda h, *_: (0, 0))]
            + [pl.BlockSpec((None, None, rows, width), lambda h, *_: (2, h, 0, 0))] * ulysses
            + [frame_spec] * 3
            + [ANYWHERE] * (len(filled) + len(after)),
            out_specs=[pl.BlockSpec((None, rows, width), lambda h, *_: (place + h, 0, 0))] * ulysses,
            scratch_shapes=[
                pltpu.VMEM((3 * frame_rows, width), jnp.bfloat16),
                pltpu.VMEM((3 * frame_rows, width), jnp.bfloat16),
                pltpu.VMEM((frame_rows + tile, width), jnp.bfloat16),
                pltpu.VMEM((frame_tiles + 1, tile, tile), jnp.float32),
                pltpu.VMEM((frame_tiles + 1, tile, tile), jnp.float32),
                pltpu.VMEM((frame_tiles + 1, tile, width), jnp.float32),
            ]
            + [pltpu.VMEM((tile, span), jnp.float32)] * ring,
        ),
        out_shape=[jax.ShapeDtypeStruct((total_heads, rows, width), jnp.bfloat16)] * ulysses,
        input_output_aliases={6 + ulysses + k: k for k in range(len(filled))},
        compiler_params=pltpu.CompilerParams(vmem_limit_bytes=60 << 20),
        cost_estimate=pl.CostEstimate(flops=0, bytes_accessed=1 << 20, transcendentals=0),
        name="attend",
    )(units, unit_count, signs, *queries, near, current, far, *filled, *after)


def across(block, step):
    size = lax.axis_size("uly")
    return lax.ppermute(block, "uly", [(i, i ^ step) for i in range(size)])


def swapped(block, odd):
    size = lax.axis_size("blk")
    pairs = [(i, i + 1) for i in range(odd, size - 1, 2)]
    return lax.ppermute(block, "blk", pairs + [(b, a) for a, b in pairs])


def shards(q_code, k_code, v_code, block_exp, window, window_count):
    rows, model_width = q_code.shape
    tile = rows // block_exp.shape[0]
    head_count = block_exp.shape[2]
    width = model_width // head_count
    ulysses = lax.axis_size("uly")
    local_heads = head_count // ulysses
    place = lax.axis_index("uly").astype(jnp.int32)
    z = place.reshape(1)
    factor = jnp.exp2(block_exp.astype(jnp.float32))
    signs = hadamard_signs(width)
    sizes, shared = cut(local_heads)
    firsts = [sum(sizes[:c]) for c in range(len(sizes))]
    steps = len(sizes)
    odd = lax.axis_index("blk").astype(jnp.int32) % 2
    units, unit_count = unit_table(window, window_count, place, odd, rows // tile, GROUP)
    arrived, halos, returned = {}, {}, []
    last = []
    ends = [sum(shared[: g + 1]) for g in range(len(shared))]
    filled, group_first, heads_before = [], 0, []

    def send(c):
        nonlocal last
        packed = pack(
            z, factor, q_code, k_code, v_code, firsts[c], sizes[c], local_heads, width, ulysses, tile, last
        )
        last = [packed[0]]
        arrived[c] = [packed[0]] + [across(packed[k], k) for k in range(1, ulysses)]

    def spread(c):
        nonlocal last
        current = join(arrived[c], last)
        last = [current]
        halos[c] = (swapped(current, 0), current, swapped(current, 1))

    def compute(c):
        nonlocal last, filled, group_first
        group_end = min(end for end in ends if end > c)
        total_heads = sum(sizes[group_first:group_end])
        filled = attend(
            units, unit_count, signs, arrived[c], *halos[c], filled,
            firsts[c] - firsts[group_first], total_heads, width, tile, GROUP, last,
        )
        last = [filled[0]]
        if c + 1 == group_end:
            returned.append([filled[0]] + [across(filled[k], k) for k in range(1, ulysses)])
            heads_before.append(firsts[group_first])
            filled, group_first = [], group_end

    for c in range(min(AHEAD, steps)):
        send(c)
    for c in range(steps):
        spread(c)
        if c + AHEAD < steps:
            send(c + AHEAD)
        if c >= 1:
            compute(c - 1)
    compute(steps - 1)
    return collect(z, returned, heads_before, local_heads, tile)


def solution(mesh):
    return jax.shard_map(
        shards,
        mesh=mesh,
        in_specs=(
            P(("blk", "uly"), None),
            P(("blk", "uly"), None),
            P(("blk", "uly"), None),
            P(("blk", "uly"), None, None),
            P("blk", None),
            P("blk"),
        ),
        out_specs=P(("blk", "uly"), None),
        check_vma=False,
    )
```

```python
import math

import jax
import jax.numpy as jnp
from jax import lax
from jax.experimental import pallas as pl
from jax.experimental.pallas import tpu as pltpu
from jax.sharding import PartitionSpec as P

LOG2E = math.log2(math.e)
ANYWHERE = pl.BlockSpec(memory_space=pl.ANY)
GROUP = 9
VMEM = 60 << 20
STEPS = 6
BACK = (2, 3, 1)
AHEAD = 2


def hadamard_signs(order):
    indices = jnp.arange(order, dtype=jnp.int32)
    common = indices[:, None] & indices[None, :]
    parity = jnp.zeros((order, order), jnp.int32)
    for bit_pos in range(max(1, order.bit_length())):
        parity = parity + (common >> bit_pos & 1)
    return jnp.where(parity % 2 == 0, 1.0, -1.0).astype(jnp.bfloat16)


def cut(local_heads):
    if local_heads % STEPS == 0:
        return [local_heads // STEPS] * STEPS, BACK
    return [1] * local_heads, [1] * local_heads


def params():
    return pltpu.CompilerParams(vmem_limit_bytes=VMEM)


def light():
    return pl.CostEstimate(flops=0, bytes_accessed=1 << 20, transcendentals=0)


def pack(z, factor, q_code, k_code, v_code, first, heads, local_heads, width, ulysses, tile, after):
    rows = q_code.shape[0]

    def body(z_ref, factor_ref, *refs):
        codes = refs[: 3 * ulysses]
        outs = refs[-ulysses:]
        for k in range(ulysses):
            head = (z_ref[0] ^ k) * local_heads + first + pl.program_id(0)
            for part, column in enumerate((1, 2, 0)):
                for i in range(rows // tile):
                    span = slice(i * tile, (i + 1) * tile)
                    block = codes[3 * k + part][span, :].astype(jnp.float32) * factor_ref[i, column, head]
                    outs[k][part, span, :] = block.astype(jnp.bfloat16)

    in_specs = [pl.BlockSpec(memory_space=pltpu.SMEM)]
    operands = [factor]
    for k in range(ulysses):
        spec = pl.BlockSpec((rows, width), lambda h, z_ref, k=k: (0, (z_ref[0] ^ k) * local_heads + first + h))
        in_specs += [spec] * 3
        operands += [k_code, v_code, q_code]
    return pl.pallas_call(
        body,
        grid_spec=pltpu.PrefetchScalarGridSpec(
            num_scalar_prefetch=1,
            grid=(heads,),
            in_specs=in_specs + [ANYWHERE] * len(after),
            out_specs=[pl.BlockSpec((3, None, rows, width), lambda h, z_ref: (0, h, 0, 0))] * ulysses,
        ),
        out_shape=[jax.ShapeDtypeStruct((3, heads, rows, width), jnp.bfloat16)] * ulysses,
        compiler_params=params(),
        cost_estimate=light(),
        name="pack",
    )(z, *operands, *after)


def join(pieces, after):
    count = len(pieces)
    _, heads, rows, width = pieces[0].shape

    def body(*refs):
        out = refs[-1]
        for k in range(count):
            out[pl.ds(k * rows, rows), :] = refs[k][...]

    return pl.pallas_call(
        body,
        grid=(heads, 2),
        in_specs=[pl.BlockSpec((None, None, rows, width), lambda h, p: (p, h, 0, 0))] * count
        + [ANYWHERE] * len(after),
        out_specs=pl.BlockSpec((None, None, count * rows, width), lambda h, p: (h, p, 0, 0)),
        out_shape=jax.ShapeDtypeStruct((heads, 2, count * rows, width), jnp.bfloat16),
        compiler_params=params(),
        cost_estimate=light(),
        name="join",
    )(*pieces, *after)


def collect(z, returned, heads_before, local_heads, tile):
    ulysses = len(returned[0])
    _, rows, width = returned[0][0].shape
    model_width = ulysses * local_heads * width
    pieces = [(c, k) for c in range(len(returned)) for k in range(ulysses)]

    def body(z_ref, *refs):
        out = refs[-1]
        for ref, (c, k) in zip(refs, pieces):
            for h in range(ref.shape[0]):
                column = ((z_ref[0] ^ k) * local_heads + heads_before[c] + h) * width
                out[:, pl.ds(pl.multiple_of(column, width), width)] = ref[h]

    return pl.pallas_call(
        body,
        grid_spec=pltpu.PrefetchScalarGridSpec(
            num_scalar_prefetch=1,
            grid=(rows // tile,),
            in_specs=[
                pl.BlockSpec((returned[c][k].shape[0], tile, width), lambda i, z_ref: (0, i, 0))
                for c, k in pieces
            ],
            out_specs=pl.BlockSpec((tile, model_width), lambda i, z_ref: (i, 0)),
        ),
        out_shape=jax.ShapeDtypeStruct((rows, model_width), jnp.bfloat16),
        compiler_params=params(),
        cost_estimate=light(),
        name="collect",
    )(z, *[returned[c][k] for c, k in pieces])


def unit_table(window, window_count, z, odd, per_piece, group):
    frame_tiles, slot_total = window.shape
    groups = window_count // group
    ends = jnp.cumsum(groups)
    unit = jnp.arange(frame_tiles * (slot_total // group) + 16, dtype=jnp.int32)
    owner = jnp.sum(unit[:, None] >= ends[None, :], axis=1).astype(jnp.int32)
    order = jnp.minimum(unit - (ends - groups)[jnp.minimum(owner, frame_tiles - 1)], slot_total // group - 1)

    def placed(tiles):
        frame, inside = tiles // frame_tiles, tiles % frame_tiles
        slot = jnp.where(frame == 1, 1, jnp.where(odd == 1, frame, 2 - frame))
        return slot * frame_tiles + ((inside // per_piece) ^ z) * per_piece + inside % per_piece

    members = placed(window).reshape(frame_tiles, slot_total // group, group)
    members = members[jnp.minimum(owner, frame_tiles - 1), order]
    spare = owner >= frame_tiles
    inside = jnp.minimum(owner, frame_tiles - 1)
    own = jnp.where(spare, frame_tiles, ((inside // per_piece) ^ z) * per_piece + inside % per_piece)
    first = (order == 0) | spare
    head = jnp.stack([own, first.astype(jnp.int32)], axis=1)
    return jnp.concatenate([head, members], axis=1).reshape(-1), ends[-1:]


def attend(units, unit_count, signs, queries, near, current, far, filled, place, total_heads, width, tile, group, after):
    ulysses = len(queries)
    heads, _, frame_rows, _ = current.shape
    rows = frame_rows // ulysses
    frame_tiles = frame_rows // tile
    span = group * tile
    stride = group + 2
    lag, ring, batch = 6, 8, 4
    to_log2 = LOG2E / math.sqrt(width)
    post = 1.0 / math.sqrt(width)

    def body(unit_ref, count_ref, signs_ref, *refs):
        query_refs = refs[:ulysses]
        frames = refs[ulysses : ulysses + 3]
        refs = refs[ulysses + 3 + len(filled) + len(after) :]
        outs = refs[:ulysses]
        keys, values, query_all, tops, total_all, sum_all = refs[ulysses : ulysses + 6]
        scores = refs[ulysses + 6 :]
        count = count_ref[0]
        for k in range(ulysses):
            query_all[pl.ds(k * rows, rows), :] = query_refs[k][...]
        for f in range(3):
            values[pl.ds(f * frame_rows, frame_rows), :] = frames[f][1]
            keys[pl.ds(f * frame_rows, frame_rows), :] = frames[f][0]
        total_all[...] = jnp.zeros_like(total_all)
        sum_all[...] = jnp.zeros_like(sum_all)

        def tiles_of(source, u):
            parts = []
            for s in range(group):
                start = pl.multiple_of(unit_ref[u * stride + 2 + s] * tile, tile)
                parts.append(source[pl.ds(start, tile), :])
            return jnp.concatenate(parts, axis=0)

        def score(u, slot):
            t = unit_ref[u * stride]
            query = query_all[pl.ds(pl.multiple_of(t * tile, tile), tile), :]
            block = lax.dot_general(
                query, tiles_of(keys, u), (((1,), (1,)), ((), ())), preferred_element_type=jnp.float32
            )
            scores[slot][...] = block
            top = block[:, :tile]
            for s in range(1, group):
                top = jnp.maximum(top, block[:, s * tile : (s + 1) * tile])
            known = tops[t]
            tops[t] = jnp.where(unit_ref[u * stride + 1] == 1, top, jnp.maximum(top, known))

        def weigh(u, slot, top):
            t = unit_ref[u * stride]
            expo = jnp.exp2(scores[slot][...] * to_log2 - top)
            total = expo[:, :tile]
            for s in range(1, group):
                total = total + expo[:, s * tile : (s + 1) * tile]
            place = pl.ds(pl.multiple_of(t * tile, tile), tile)
            total_all[place, :] += total
            sum_all[place, :] += lax.dot_general(
                expo.astype(jnp.bfloat16),
                tiles_of(values, u),
                (((1,), (0,)), ((), ())),
                preferred_element_type=jnp.float32,
            )

        for u in range(lag):
            score(u, u)

        def one_batch(u, slot):
            most = [
                jnp.max(tops[unit_ref[(u + j) * stride]], axis=1, keepdims=True) * to_log2 for j in range(batch)
            ]
            for j in range(batch):
                score(u + j + lag, (slot + j + lag) % ring)
                weigh(u + j, slot + j, most[j])

        def two_batches(i, carry):
            one_batch(i * ring, 0)

            @pl.when(i * ring + batch < count)
            def _():
                one_batch(i * ring + batch, batch)

            return carry

        lax.fori_loop(0, (count + ring - 1) // ring, two_batches, 0)
        for k in range(ulysses):
            part = pl.ds(k * rows, rows)
            rotated = sum_all[part, :] * (post / jnp.sum(total_all[part, :], axis=1, keepdims=True))
            high = rotated.astype(jnp.bfloat16)
            rest = rotated - high.astype(jnp.float32)
            middle = rest.astype(jnp.bfloat16)
            low = (rest - middle.astype(jnp.float32)).astype(jnp.bfloat16)
            signs_val = signs_ref[...]
            result = jnp.dot(low, signs_val, preferred_element_type=jnp.float32)
            result += jnp.dot(middle, signs_val, preferred_element_type=jnp.float32)
            result += jnp.dot(high, signs_val, preferred_element_type=jnp.float32)
            outs[k][...] = result.astype(jnp.bfloat16)

    frame_spec = pl.BlockSpec((None, 2, frame_rows, width), lambda h, *_: (h, 0, 0, 0))
    return pl.pallas_call(
        body,
        grid_spec=pltpu.PrefetchScalarGridSpec(
            num_scalar_prefetch=2,
            grid=(heads,),
            in_specs=[pl.BlockSpec((width, width), lambda h, *_: (0, 0))]
            + [pl.BlockSpec((None, None, rows, width), lambda h, *_: (2, h, 0, 0))] * ulysses
            + [frame_spec] * 3
            + [ANYWHERE] * (len(filled) + len(after)),
            out_specs=[pl.BlockSpec((None, rows, width), lambda h, *_: (place + h, 0, 0))] * ulysses,
            scratch_shapes=[
                pltpu.VMEM((3 * frame_rows, width), jnp.bfloat16),
                pltpu.VMEM((3 * frame_rows, width), jnp.bfloat16),
                pltpu.VMEM((frame_rows + tile, width), jnp.bfloat16),
                pltpu.VMEM((frame_tiles + 1, tile, tile), jnp.float32),
                pltpu.VMEM((frame_rows + tile, tile), jnp.float32),
                pltpu.VMEM((frame_rows + tile, width), jnp.float32),
            ]
            + [pltpu.VMEM((tile, span), jnp.float32)] * ring,
        ),
        out_shape=[jax.ShapeDtypeStruct((total_heads, rows, width), jnp.bfloat16)] * ulysses,
        input_output_aliases={6 + ulysses + k: k for k in range(len(filled))},
        compiler_params=pltpu.CompilerParams(vmem_limit_bytes=60 << 20),
        cost_estimate=pl.CostEstimate(flops=0, bytes_accessed=1 << 20, transcendentals=0),
        name="attend",
    )(units, unit_count, signs, *queries, near, current, far, *filled, *after)


def across(block, step):
    size = lax.axis_size("uly")
    return lax.ppermute(block, "uly", [(i, i ^ step) for i in range(size)])


def swapped(block, odd):
    size = lax.axis_size("blk")
    pairs = [(i, i + 1) for i in range(odd, size - 1, 2)]
    return lax.ppermute(block, "blk", pairs + [(b, a) for a, b in pairs])


def shards(q_code, k_code, v_code, block_exp, window, window_count):
    rows, model_width = q_code.shape
    tile = rows // block_exp.shape[0]
    head_count = block_exp.shape[2]
    width = model_width // head_count
    ulysses = lax.axis_size("uly")
    local_heads = head_count // ulysses
    place = lax.axis_index("uly").astype(jnp.int32)
    z = place.reshape(1)
    factor = jnp.exp2(block_exp.astype(jnp.float32))
    signs = hadamard_signs(width)
    sizes, shared = cut(local_heads)
    firsts = [sum(sizes[:c]) for c in range(len(sizes))]
    steps = len(sizes)
    odd = lax.axis_index("blk").astype(jnp.int32) % 2
    units, unit_count = unit_table(window, window_count, place, odd, rows // tile, GROUP)
    arrived, halos, returned = {}, {}, []
    last = []
    ends = [sum(shared[: g + 1]) for g in range(len(shared))]
    filled, group_first, heads_before = [], 0, []

    def send(c):
        nonlocal last
        packed = pack(
            z, factor, q_code, k_code, v_code, firsts[c], sizes[c], local_heads, width, ulysses, tile, last
        )
        last = [packed[0]]
        arrived[c] = [packed[0]] + [across(packed[k], k) for k in range(1, ulysses)]

    def spread(c):
        nonlocal last
        current = join(arrived[c], last)
        last = [current]
        halos[c] = (swapped(current, 0), current, swapped(current, 1))

    def compute(c):
        nonlocal last, filled, group_first
        group_end = min(end for end in ends if end > c)
        total_heads = sum(sizes[group_first:group_end])
        filled = attend(
            units, unit_count, signs, arrived[c], *halos[c], filled,
            firsts[c] - firsts[group_first], total_heads, width, tile, GROUP, last,
        )
        last = [filled[0]]
        if c + 1 == group_end:
            returned.append([filled[0]] + [across(filled[k], k) for k in range(1, ulysses)])
            heads_before.append(firsts[group_first])
            filled, group_first = [], group_end

    for c in range(min(AHEAD, steps)):
        send(c)
    for c in range(steps):
        spread(c)
        if c + AHEAD < steps:
            send(c + AHEAD)
        if c >= 1:
            compute(c - 1)
    compute(steps - 1)
    return collect(z, returned, heads_before, local_heads, tile)


def solution(mesh):
    return jax.shard_map(
        shards,
        mesh=mesh,
        in_specs=(
            P(("blk", "uly"), None),
            P(("blk", "uly"), None),
            P(("blk", "uly"), None),
            P(("blk", "uly"), None, None),
            P("blk", None),
            P("blk"),
        ),
        out_specs=P(("blk", "uly"), None),
        check_vma=False,
    )
```

```python
import math

import jax
import jax.numpy as jnp
from jax import lax
from jax.experimental import pallas as pl
from jax.experimental.pallas import tpu as pltpu
from jax.sharding import PartitionSpec as P

LOG2E = math.log2(math.e)
ANYWHERE = pl.BlockSpec(memory_space=pl.ANY)
GROUP = 9
VMEM = 60 << 20
STEPS = 6
BACK = (2, 3, 1)
AHEAD = 2


def hadamard_signs(order):
    indices = jnp.arange(order, dtype=jnp.int32)
    common = indices[:, None] & indices[None, :]
    parity = jnp.zeros((order, order), jnp.int32)
    for bit_pos in range(max(1, order.bit_length())):
        parity = parity + (common >> bit_pos & 1)
    return jnp.where(parity % 2 == 0, 1.0, -1.0).astype(jnp.bfloat16)


def cut(local_heads):
    if local_heads % STEPS == 0:
        return [local_heads // STEPS] * STEPS, BACK
    return [1] * local_heads, [1] * local_heads


def params():
    return pltpu.CompilerParams(vmem_limit_bytes=VMEM)


def light():
    return pl.CostEstimate(flops=0, bytes_accessed=1 << 20, transcendentals=0)


def pack(z, factor, q_code, k_code, v_code, first, heads, local_heads, width, ulysses, tile, after):
    rows = q_code.shape[0]

    def body(z_ref, factor_ref, *refs):
        codes = refs[: 3 * ulysses]
        outs = refs[-ulysses:]
        for k in range(ulysses):
            head = (z_ref[0] ^ k) * local_heads + first + pl.program_id(0)
            for part, column in enumerate((1, 2, 0)):
                for i in range(rows // tile):
                    span = slice(i * tile, (i + 1) * tile)
                    block = codes[3 * k + part][span, :].astype(jnp.float32) * factor_ref[i, column, head]
                    outs[k][part, span, :] = block.astype(jnp.bfloat16)

    in_specs = [pl.BlockSpec(memory_space=pltpu.SMEM)]
    operands = [factor]
    for k in range(ulysses):
        spec = pl.BlockSpec((rows, width), lambda h, z_ref, k=k: (0, (z_ref[0] ^ k) * local_heads + first + h))
        in_specs += [spec] * 3
        operands += [k_code, v_code, q_code]
    return pl.pallas_call(
        body,
        grid_spec=pltpu.PrefetchScalarGridSpec(
            num_scalar_prefetch=1,
            grid=(heads,),
            in_specs=in_specs + [ANYWHERE] * len(after),
            out_specs=[pl.BlockSpec((3, None, rows, width), lambda h, z_ref: (0, h, 0, 0))] * ulysses,
        ),
        out_shape=[jax.ShapeDtypeStruct((3, heads, rows, width), jnp.bfloat16)] * ulysses,
        compiler_params=params(),
        cost_estimate=light(),
        name="pack",
    )(z, *operands, *after)


def join(pieces, after):
    count = len(pieces)
    _, heads, rows, width = pieces[0].shape

    def body(*refs):
        out = refs[-1]
        for k in range(count):
            out[pl.ds(k * rows, rows), :] = refs[k][...]

    return pl.pallas_call(
        body,
        grid=(heads, 2),
        in_specs=[pl.BlockSpec((None, None, rows, width), lambda h, p: (p, h, 0, 0))] * count
        + [ANYWHERE] * len(after),
        out_specs=pl.BlockSpec((None, None, count * rows, width), lambda h, p: (h, p, 0, 0)),
        out_shape=jax.ShapeDtypeStruct((heads, 2, count * rows, width), jnp.bfloat16),
        compiler_params=params(),
        cost_estimate=light(),
        name="join",
    )(*pieces, *after)


def collect(z, returned, heads_before, local_heads, tile):
    ulysses = len(returned[0])
    _, rows, width = returned[0][0].shape
    model_width = ulysses * local_heads * width
    pieces = [(c, k) for c in range(len(returned)) for k in range(ulysses)]

    def body(z_ref, *refs):
        out = refs[-1]
        for ref, (c, k) in zip(refs, pieces):
            for h in range(ref.shape[0]):
                column = ((z_ref[0] ^ k) * local_heads + heads_before[c] + h) * width
                out[:, pl.ds(pl.multiple_of(column, width), width)] = ref[h]

    return pl.pallas_call(
        body,
        grid_spec=pltpu.PrefetchScalarGridSpec(
            num_scalar_prefetch=1,
            grid=(rows // tile,),
            in_specs=[
                pl.BlockSpec((returned[c][k].shape[0], tile, width), lambda i, z_ref: (0, i, 0))
                for c, k in pieces
            ],
            out_specs=pl.BlockSpec((tile, model_width), lambda i, z_ref: (i, 0)),
        ),
        out_shape=jax.ShapeDtypeStruct((rows, model_width), jnp.bfloat16),
        compiler_params=params(),
        cost_estimate=light(),
        name="collect",
    )(z, *[returned[c][k] for c, k in pieces])


def unit_table(window, window_count, z, odd, per_piece, group):
    frame_tiles, slot_total = window.shape
    groups = window_count // group
    ends = jnp.cumsum(groups)
    unit = jnp.arange(frame_tiles * (slot_total // group) + 16, dtype=jnp.int32)
    owner = jnp.sum(unit[:, None] >= ends[None, :], axis=1).astype(jnp.int32)
    order = jnp.minimum(unit - (ends - groups)[jnp.minimum(owner, frame_tiles - 1)], slot_total // group - 1)

    def placed(tiles):
        frame, inside = tiles // frame_tiles, tiles % frame_tiles
        slot = jnp.where(frame == 1, 1, jnp.where(odd == 1, frame, 2 - frame))
        return slot * frame_tiles + ((inside // per_piece) ^ z) * per_piece + inside % per_piece

    members = placed(window).reshape(frame_tiles, slot_total // group, group)
    members = members[jnp.minimum(owner, frame_tiles - 1), order]
    spare = owner >= frame_tiles
    inside = jnp.minimum(owner, frame_tiles - 1)
    own = jnp.where(spare, frame_tiles, ((inside // per_piece) ^ z) * per_piece + inside % per_piece)
    first = (order == 0) | spare
    head = jnp.stack([own, first.astype(jnp.int32)], axis=1)
    return jnp.concatenate([head, members], axis=1).reshape(-1), ends[-1:]


def attend(units, unit_count, signs, queries, near, current, far, filled, place, total_heads, width, tile, group, after):
    ulysses = len(queries)
    heads, _, frame_rows, _ = current.shape
    rows = frame_rows // ulysses
    frame_tiles = frame_rows // tile
    span = group * tile
    stride = group + 2
    lag, ring, batch = 6, 8, 4
    to_log2 = LOG2E / math.sqrt(width)
    post = 1.0 / math.sqrt(width)

    def body(unit_ref, count_ref, signs_ref, *refs):
        query_refs = refs[:ulysses]
        frames = refs[ulysses : ulysses + 3]
        refs = refs[ulysses + 3 + len(filled) + len(after) :]
        outs = refs[:ulysses]
        keys, values, query_all, tops, total_all, sum_all = refs[ulysses : ulysses + 6]
        scores = refs[ulysses + 6 :]
        count = count_ref[0]
        for k in range(ulysses):
            query_all[pl.ds(k * rows, rows), :] = query_refs[k][...]
        for f in range(3):
            values[pl.ds(f * frame_rows, frame_rows), :] = frames[f][1]
            keys[pl.ds(f * frame_rows, frame_rows), :] = frames[f][0]
        total_all[...] = jnp.zeros_like(total_all)
        sum_all[...] = jnp.zeros_like(sum_all)

        def tiles_of(source, u):
            parts = []
            for s in range(group):
                start = pl.multiple_of(unit_ref[u * stride + 2 + s] * tile, tile)
                parts.append(source[pl.ds(start, tile), :])
            return jnp.concatenate(parts, axis=0)

        def score(u, slot):
            t = unit_ref[u * stride]
            query = query_all[pl.ds(pl.multiple_of(t * tile, tile), tile), :]
            block = lax.dot_general(
                query, tiles_of(keys, u), (((1,), (1,)), ((), ())), preferred_element_type=jnp.float32
            )
            scores[slot][...] = block
            top = block[:, :tile]
            for s in range(1, group):
                top = jnp.maximum(top, block[:, s * tile : (s + 1) * tile])
            known = tops[t]
            tops[t] = jnp.where(unit_ref[u * stride + 1] == 1, top, jnp.maximum(top, known))

        def weigh(u, slot, top):
            t = unit_ref[u * stride]
            expo = jnp.exp2(scores[slot][...] * to_log2 - top)
            total = expo[:, :tile]
            for s in range(1, group):
                total = total + expo[:, s * tile : (s + 1) * tile]
            place = pl.ds(pl.multiple_of(t * tile, tile), tile)
            total_all[place, :] += total
            sum_all[place, :] += lax.dot_general(
                expo.astype(jnp.bfloat16),
                tiles_of(values, u),
                (((1,), (0,)), ((), ())),
                preferred_element_type=jnp.float32,
            )

        for u in range(lag):
            score(u, u)

        def one_batch(u, slot):
            most = [
                jnp.max(tops[unit_ref[(u + j) * stride]], axis=1, keepdims=True) * to_log2 for j in range(batch)
            ]
            for j in range(batch):
                score(u + j + lag, (slot + j + lag) % ring)
                weigh(u + j, slot + j, most[j])

        def two_batches(i, carry):
            one_batch(i * ring, 0)

            @pl.when(i * ring + batch < count)
            def _():
                one_batch(i * ring + batch, batch)

            return carry

        lax.fori_loop(0, (count + ring - 1) // ring, two_batches, 0)
        for k in range(ulysses):
            part = pl.ds(k * rows, rows)
            rotated = sum_all[part, :] * (post / jnp.sum(total_all[part, :], axis=1, keepdims=True))
            high = rotated.astype(jnp.bfloat16)
            rest = rotated - high.astype(jnp.float32)
            middle = rest.astype(jnp.bfloat16)
            low = (rest - middle.astype(jnp.float32)).astype(jnp.bfloat16)
            signs_val = signs_ref[...]
            result = jnp.dot(low, signs_val, preferred_element_type=jnp.float32)
            result += jnp.dot(middle, signs_val, preferred_element_type=jnp.float32)
            result += jnp.dot(high, signs_val, preferred_element_type=jnp.float32)
            outs[k][...] = result.astype(jnp.bfloat16)

    frame_spec = pl.BlockSpec((None, 2, frame_rows, width), lambda h, *_: (h, 0, 0, 0))
    return pl.pallas_call(
        body,
        grid_spec=pltpu.PrefetchScalarGridSpec(
            num_scalar_prefetch=2,
            grid=(heads,),
            in_specs=[pl.BlockSpec((width, width), lambda h, *_: (0, 0))]
            + [pl.BlockSpec((None, None, rows, width), lambda h, *_: (2, h, 0, 0))] * ulysses
            + [frame_spec] * 3
            + [ANYWHERE] * (len(filled) + len(after)),
            out_specs=[pl.BlockSpec((None, rows, width), lambda h, *_: (place + h, 0, 0))] * ulysses,
            scratch_shapes=[
                pltpu.VMEM((3 * frame_rows, width), jnp.bfloat16),
                pltpu.VMEM((3 * frame_rows, width), jnp.bfloat16),
                pltpu.VMEM((frame_rows + tile, width), jnp.bfloat16),
                pltpu.VMEM((frame_tiles + 1, tile, tile), jnp.float32),
                pltpu.VMEM((frame_rows + tile, tile), jnp.float32),
                pltpu.VMEM((frame_rows + tile, width), jnp.float32),
            ]
            + [pltpu.VMEM((tile, span), jnp.float32)] * ring,
        ),
        out_shape=[jax.ShapeDtypeStruct((total_heads, rows, width), jnp.bfloat16)] * ulysses,
        input_output_aliases={6 + ulysses + k: k for k in range(len(filled))},
        compiler_params=pltpu.CompilerParams(vmem_limit_bytes=60 << 20),
        cost_estimate=pl.CostEstimate(flops=0, bytes_accessed=1 << 20, transcendentals=0),
        name="attend",
    )(units, unit_count, signs, *queries, near, current, far, *filled, *after)


def across(block, step):
    size = lax.axis_size("uly")
    return lax.ppermute(block, "uly", [(i, i ^ step) for i in range(size)])


def swapped(block, odd):
    size = lax.axis_size("blk")
    pairs = [(i, i + 1) for i in range(odd, size - 1, 2)]
    return lax.ppermute(block, "blk", pairs + [(b, a) for a, b in pairs])


def shards(q_code, k_code, v_code, block_exp, window, window_count):
    rows, model_width = q_code.shape
    tile = rows // block_exp.shape[0]
    head_count = block_exp.shape[2]
    width = model_width // head_count
    ulysses = lax.axis_size("uly")
    local_heads = head_count // ulysses
    place = lax.axis_index("uly").astype(jnp.int32)
    z = place.reshape(1)
    factor = jnp.exp2(block_exp.astype(jnp.float32))
    signs = hadamard_signs(width)
    sizes, shared = cut(local_heads)
    firsts = [sum(sizes[:c]) for c in range(len(sizes))]
    steps = len(sizes)
    odd = lax.axis_index("blk").astype(jnp.int32) % 2
    units, unit_count = unit_table(window, window_count, place, odd, rows // tile, GROUP)
    arrived, halos, returned = {}, {}, []
    last = []
    ends = [sum(shared[: g + 1]) for g in range(len(shared))]
    filled, group_first, heads_before = [], 0, []

    def send(c):
        nonlocal last
        packed = pack(
            z, factor, q_code, k_code, v_code, firsts[c], sizes[c], local_heads, width, ulysses, tile, last
        )
        last = [packed[0]]
        arrived[c] = [packed[0]] + [across(packed[k], k) for k in range(1, ulysses)]

    def spread(c):
        nonlocal last
        current = join(arrived[c], last)
        last = [current]
        halos[c] = (swapped(current, 0), current, swapped(current, 1))

    def compute(c):
        nonlocal last, filled, group_first
        group_end = min(end for end in ends if end > c)
        total_heads = sum(sizes[group_first:group_end])
        filled = attend(
            units, unit_count, signs, arrived[c], *halos[c], filled,
            firsts[c] - firsts[group_first], total_heads, width, tile, GROUP, last,
        )
        last = [filled[0]]
        if c + 1 == group_end:
            returned.append([filled[0]] + [across(filled[k], k) for k in range(1, ulysses)])
            heads_before.append(firsts[group_first])
            filled, group_first = [], group_end

    for c in range(min(AHEAD, steps)):
        send(c)
    for c in range(steps):
        spread(c)
        if c + AHEAD < steps:
            send(c + AHEAD)
        if c >= 1:
            compute(c - 1)
    compute(steps - 1)
    return collect(z, returned, heads_before, local_heads, min(rows, 2 * tile))


def solution(mesh):
    return jax.shard_map(
        shards,
        mesh=mesh,
        in_specs=(
            P(("blk", "uly"), None),
            P(("blk", "uly"), None),
            P(("blk", "uly"), None),
            P(("blk", "uly"), None, None),
            P("blk", None),
            P("blk"),
        ),
        out_specs=P(("blk", "uly"), None),
        check_vma=False,
    )
```
